32 devices in a mesh: seq: 16 (over z, x, core), exp: 2 (over y).
Axes of the slice: x: 2, y: 2, z: 4, core: 2. Of those that a mesh axis runs over, the one named last changes fastest.
Arguments:
- queries: bfloat16 [1024, 6144], P('seq', 'exp'), may hold values from -6 to 6
- keys: bfloat16 [1024, 6144], P('seq', 'exp'), may hold values from -6 to 6
- values: bfloat16 [1024, 6144], P('seq', 'exp'), may hold values from -6 to 6
- log_decay: float32 [48, 1024], P('exp', 'seq'), may hold values from -1 to 0
- state_in: float32 [48, 128, 128], P('exp'), may hold values from -24 to 24
- norm_gain: float32 [6144], replicated, may hold values from 0.1 to 1.9
- routes: int32 [1024, 2], P('seq'), may hold values from 0 to 7, all different within a row; in each aligned block of 64 rows (0 to 63, 64 to 127, ...) at most 20 rows name the same one
- w_gate: bfloat16 [8, 9216, 6144], P('exp', 'seq'), may hold values from -0.078125 to 0.078125
- w_up: bfloat16 [8, 9216, 6144], P('exp', 'seq'), may hold values from -0.078125 to 0.078125
Outputs:
- expert_hidden: bfloat16 [8, 9216, 320], P('exp', 'seq')
- state_out: float32 [48, 128, 128], P('exp', 'seq')
The draws below stay inside these ranges and needn't reach their ends.
Inputs may be any that keep to these rules, and one draw needn't show every extreme that they name: `routes`: each token names two different experts; in each aligned block of 64 tokens no expert is named by more than 20 tokens, and some blocks reach exactly 20.
All inputs are finite; a program needn't handle non-finite values.
Results may differ from the reference program's by a relative error of at most 0.0071.
Values may be sent and summed in bfloat16 or wider, within the bound.
No kernel may reach another device: no remote copies, remote signals or barrier semaphores. Data moves between devices by JAX's collectives and lax.ppermute only.
A program may use at most 128 MiB of HBM per device.

```python
import math
import jax
import jax.numpy as jnp
import numpy as np
from jax import lax

QUERY_GROUP_COUNT = 48
HEAD_DIM = 128
D = 6144
FF = 9216
EXPERTS = 8
TOK_BLK = 64
CAP = 20
PROMPT_LENGTH = 1024
SLOTS = 320
N_SEQ = 16


def draw_log_decay(key, part):
    generator_children = jax.random.split(key, 5)
    picker = jax.random.uniform(generator_children[0], (QUERY_GROUP_COUNT, 1))
    level = jax.random.uniform(generator_children[1], (QUERY_GROUP_COUNT, 1))
    slow_rate = jnp.exp(jnp.log(1.0 / (4.0 * PROMPT_LENGTH)) + level * jnp.log(4.0))
    fast_rate = jnp.exp(jnp.log(1.0 / PROMPT_LENGTH) + level * jnp.log(PROMPT_LENGTH / 30.0))
    forgetting_factor = jnp.where(picker < 0.5, slow_rate, fast_rate)
    stochastic_perturbation = jnp.exp(jax.random.uniform(generator_children[2], (QUERY_GROUP_COUNT, PROMPT_LENGTH), minval=jnp.log(0.5), maxval=jnp.log(2.0)))
    spike_occurrences = jax.random.uniform(generator_children[3], (QUERY_GROUP_COUNT, PROMPT_LENGTH)) < 3.0 / PROMPT_LENGTH
    objective_samples = jnp.log(jax.random.uniform(generator_children[4], (QUERY_GROUP_COUNT, PROMPT_LENGTH), minval=0.5, maxval=0.8))
    return (-forgetting_factor * stochastic_perturbation + jnp.where(spike_occurrences, objective_samples, 0.0)).astype(jnp.float32)


def level_of(own_key, extent, pieces, least, high):
    def one(axis_at, shards_of):
        heights = jax.random.uniform(jax.random.fold_in(jax.random.fold_in(own_key, 6), axis_at), (shards_of,), jnp.float32, least / len(pieces), high / len(pieces))
        return jnp.repeat(jnp.exp(heights), extent[axis_at] // shards_of).reshape((-1,) + (1,) * (len(extent) - axis_at - 1))

    factor_of = one(*pieces[0])
    for cut in pieces[1:]:
        factor_of = factor_of * one(*cut)
    return factor_of


def assign_block(key, own, number, rows, number_of, top, limit, slope):
    ranking = jax.random.permutation(key, number_of)
    crowded, ordinary = shares(number_of, rows * top, limit, slope, True), shares(number_of, rows * top, limit, slope, False)
    places = jnp.arange(number_of)

    def named(sizes, turn):
        used = int((sizes > 0).sum())
        fixed = max(1, used // 4)
        moved = fixed + (places - fixed + turn * (used - fixed)) % max(1, number_of - fixed)
        return jnp.zeros((number_of,), jnp.int32).at[ranking[jnp.where(places < fixed, places, moved)]].set(jnp.asarray(sizes, jnp.int32))

    sizes = jnp.where(number % 4 == 0, named(crowded, number // 4), named(ordinary, number - number // 4 - 1))
    mixed = jax.random.permutation(jax.random.fold_in(own, 3), number_of)
    giver, sink = mixed[0:number_of // 2 * 2:2], mixed[1:number_of // 2 * 2:2]
    room = jnp.minimum(sizes[giver] - 1, limit - sizes[sink]) // 2
    room = jnp.where((giver == ranking[0]) | (sink == ranking[0]) | (sizes[sink] == 0), 0, jnp.maximum(room, 0))
    moved = jax.random.randint(jax.random.fold_in(own, 4), (number_of // 2,), 0, 1 << 20) % (room + 1)
    sizes = sizes.at[giver].add(-moved).at[sink].add(moved)
    items = jnp.searchsorted(jnp.cumsum(sizes), jnp.arange(rows * top), side="right").astype(jnp.int32)
    listing = items.reshape(top, rows).T
    listing = listing[jax.random.permutation(jax.random.fold_in(own, 1), rows)]
    turn = jax.random.randint(jax.random.fold_in(own, 2), (rows, 1), 0, top)
    return jnp.take_along_axis(listing, (jnp.arange(top)[None, :] + turn) % top, axis=1)


def shares(count, total, reach, slope, full):
    loads = [(1 << 20) // math.isqrt(rank ** slope) + 1 for rank in range(1, count + 1)]
    largest = reach if full else min(reach, max(-(-total // count), total * loads[0] // sum(loads)))
    least = 1 if total - largest >= count - 1 else 0
    counts, surplus = [largest] + [least] * (count - 1), total - largest - least * (count - 1)
    while surplus > 0:
        movable = [i for i in range(1, count) if counts[i] < largest] or [i for i in range(1, count) if counts[i] < reach]
        pool, budget = sum([loads[i] for i in movable]), surplus
        for i in movable:
            more = min(reach - counts[i], max(1, budget * loads[i] // pool), surplus)
            counts[i] = counts[i] + more
            surplus = surplus - more
    return np.array(counts)


def scatter_about(rng, shape, width, limit, cuts=(), kind=jnp.bfloat16):
    loudness = level_of(rng, shape, cuts, -0.22, 0.18) if cuts else 1.0
    values = jax.random.normal(rng, shape, jnp.float32) * width * loudness
    return jnp.minimum(jnp.maximum(values, -limit), limit).astype(kind)


def setup_inputs(seed: int = 0) -> dict:
    key_of = jax.random.split(jax.random.key(seed), 10)
    queries = scatter_about(key_of[0], (PROMPT_LENGTH, D), 1.0, 6.0, ((0, 16), (1, 2)))
    keys = scatter_about(key_of[1], (PROMPT_LENGTH, D), 1.0, 6.0, ((0, 16), (1, 2)))
    values = scatter_about(key_of[2], (PROMPT_LENGTH, D), 1.0, 6.0, ((0, 16), (1, 2)))
    log_decay = draw_log_decay(jax.random.fold_in(key_of[9], 71), 0)
    state_in = scatter_about(key_of[4], (QUERY_GROUP_COUNT, HEAD_DIM, HEAD_DIM), 4.0, 24.0, ((0, 2),), jnp.float32)
    norm_gain = jnp.clip(1.0 + 0.18 * jax.random.normal(key_of[5], (D,), jnp.float32), 0.1, 1.9)
    routes_keys = jax.random.split(jax.random.fold_in(key_of[6], 1), PROMPT_LENGTH // TOK_BLK)
    routes_turns = jax.random.permutation(jax.random.fold_in(key_of[6], 3), PROMPT_LENGTH // TOK_BLK)
    routes = jax.vmap(lambda own, number: assign_block(jax.random.fold_in(key_of[6], 2), own, number, TOK_BLK, EXPERTS, 2, CAP, 2))(routes_keys, routes_turns).reshape((PROMPT_LENGTH, 2))
    w_gate = scatter_about(key_of[7], (EXPERTS, FF, D), D ** -0.5, 0.078125, ((0, 2), (1, 16)))
    w_up = scatter_about(key_of[8], (EXPERTS, FF, D), D ** -0.5, 0.078125, ((0, 2), (1, 16)))
    return {"queries": queries, "keys": keys, "values": values, "log_decay": log_decay, "state_in": state_in, "norm_gain": norm_gain, "routes": routes, "w_gate": w_gate, "w_up": w_up}


epsilon = 1e-06

def reference(queries, keys, values, log_decay, state_in, norm_gain, routes, w_gate, w_up):
    heads = state_in.shape[0]
    head_dim = state_in.shape[1]
    scaling = 1.0 / math.sqrt(head_dim)
    query_all = queries.reshape(N_SEQ, TOK_BLK, heads, head_dim)
    key_all = keys.reshape(N_SEQ, TOK_BLK, heads, head_dim)
    value_all = values.reshape(N_SEQ, TOK_BLK, heads, head_dim)
    log_blocks = log_decay.reshape(heads, N_SEQ, TOK_BLK).transpose(1, 0, 2)
    causal = jnp.arange(TOK_BLK)[:, None] >= jnp.arange(TOK_BLK)[None, :]

    def block_step(running, inputs):
        query_blk, key_blk, value_blk, log_blk = inputs
        cumlog = jnp.cumsum(log_blk, axis=1)
        block_log = cumlog[:, -1]
        scores = jnp.einsum('ihd,jhd->hij', query_blk.astype(jnp.float32), key_blk.astype(jnp.float32), precision=lax.Precision.HIGHEST) * scaling
        gap_log = cumlog[:, :, None] - cumlog[:, None, :]
        weights = jnp.where(causal[None], jnp.exp(jnp.where(causal[None], gap_log, 0.0)), 0.0)
        decayed = (scores * weights).astype(jnp.bfloat16)
        inside = jnp.einsum('hij,jhd->ihd', decayed.astype(jnp.float32), value_blk.astype(jnp.float32), precision=lax.Precision.HIGHEST)
        key_weighted = key_blk.astype(jnp.float32) * jnp.exp(block_log[:, None] - cumlog).T[:, :, None]
        block_state = jnp.einsum('jhd,jhe->hde', key_weighted, value_blk.astype(jnp.float32), precision=lax.Precision.HIGHEST)
        carried_in = jnp.einsum('ihd,hde->ihe', query_blk.astype(jnp.float32) * scaling, running, precision=lax.Precision.HIGHEST)
        carried_in = carried_in * jnp.exp(cumlog).T[:, :, None]
        updated = jnp.exp(block_log)[:, None, None] * running + block_state
        return (updated, inside + carried_in)
    final_state, block_outs = lax.scan(block_step, state_in, (query_all, key_all, value_all, log_blocks))
    attended = block_outs.reshape(PROMPT_LENGTH, heads * head_dim).astype(jnp.bfloat16)
    att_wide = attended.astype(jnp.float32)
    normed = (att_wide * lax.rsqrt(lax.optimization_barrier(jnp.mean(att_wide * att_wide, axis=1, keepdims=True)) + epsilon) * norm_gain).astype(jnp.bfloat16)
    blocks = jnp.arange(PROMPT_LENGTH, dtype=jnp.int32) // TOK_BLK

    def one_expert(expert_id):
        chosen = jnp.any(routes == expert_id, axis=1).astype(jnp.int32)
        position = jnp.cumsum(chosen.reshape(N_SEQ, TOK_BLK), axis=1).reshape(PROMPT_LENGTH).astype(jnp.int32) - 1
        slot_ids = jnp.where(chosen == 1, blocks * CAP + position, SLOTS).astype(jnp.int32)
        row_set = jnp.zeros((SLOTS, D), normed.dtype).at[slot_ids].set(normed, mode='drop')
        gate_act = jnp.dot(w_gate[expert_id], row_set.T, preferred_element_type=jnp.float32)
        up_act = jnp.dot(w_up[expert_id], row_set.T, preferred_element_type=jnp.float32)
        return (jax.nn.silu(gate_act) * up_act).astype(jnp.bfloat16)
    expert_hidden = lax.map(one_expert, jnp.arange(EXPERTS, dtype=jnp.int32))
    return (expert_hidden, final_state)
```

```python
import functools
import math

import jax
import jax.numpy as jnp
from jax import lax
from jax.experimental import pallas as pl
from jax.experimental.pallas import tpu as pltpu
from jax.sharding import PartitionSpec as P

CAP = 20
EPSILON = 1e-06
COLUMN_PARTS = 3
BLOCKS_A_GROUP = 4
LOG_ROWS = 16
ROUTE_ROW = 6
MIB = 1 << 20


def split_hi_lo(wide):
    hi = wide.astype(jnp.bfloat16)
    return hi, (wide - hi.astype(jnp.float32)).astype(jnp.bfloat16)


def dot_f32(a, b, dims, precision=None):
    return lax.dot_general(
        a, b, (dims, ((), ())), precision=precision, preferred_element_type=jnp.float32
    )


def pack_kernel(place_ref, q_ref, k_ref, v_ref, log_ref, *outs, group, columns):
    block = q_ref.shape[0]
    mine = place_ref[0]
    for hop in range(group):
        message, logs = outs[hop], outs[group + hop]
        dest = jnp.bitwise_xor(mine, hop)
        for part in range(COLUMN_PARTS):
            source = pl.ds(
                pl.multiple_of((part * group + dest) * columns, columns), columns
            )
            target = slice(part * columns, (part + 1) * columns)
            message[0:block, target] = q_ref[:, source]
            message[block : 2 * block, target] = k_ref[:, source]
            message[2 * block : 3 * block, target] = v_ref[:, source]
        logs[...] = log_ref[dest]


def local_kernel(place_ref, *refs, group, heads, head_dim, block):
    messages, logs = refs[:group], refs[group : 2 * group]
    q_out, inside_out, cum_out, state_out, message_out = refs[2 * group : 2 * group + 5]
    k_all, v_all, log_all = refs[2 * group + 5 :]
    mine = place_ref[0]
    length = group * block
    for hop in range(group):
        source = jnp.bitwise_xor(mine, hop)
        rows = pl.ds(pl.multiple_of(source * block, block), block)
        q_out[rows, :] = messages[hop][0:block, :]
        k_all[rows, :] = messages[hop][block : 2 * block, :]
        v_all[rows, :] = messages[hop][2 * block : 3 * block, :]
        log_all[source] = logs[hop][...]
    cumlog = jnp.zeros((log_all.shape[1], length), jnp.float32)
    laid_out = jnp.zeros((log_all.shape[1], length), jnp.float32)
    for at in range(group):
        before = lax.broadcasted_iota(jnp.int32, (block, length), 0) + at * block
        after = lax.broadcasted_iota(jnp.int32, (block, length), 1)
        cumlog = cumlog + dot_f32(
            log_all[at],
            (before <= after).astype(jnp.float32),
            ((1,), (0,)),
            lax.Precision.HIGHEST,
        )
        laid_out = laid_out + dot_f32(
            log_all[at],
            (before == after).astype(jnp.float32),
            ((1,), (0,)),
            lax.Precision.HIGHEST,
        )
    cum_columns = cumlog.T
    cum_out[...] = cum_columns
    scaling = 1.0 / math.sqrt(head_dim)
    causal = lax.broadcasted_iota(jnp.int32, (length, length), 0) >= lax.broadcasted_iota(
        jnp.int32, (length, length), 1
    )
    row_at = lax.broadcasted_iota(jnp.int32, (LOG_ROWS, head_dim), 0)
    for head in range(heads):
        span = slice(head * head_dim, (head + 1) * head_dim)
        query, key, value = q_out[:, span], k_all[:, span], v_all[:, span]
        column = cum_columns[:, head : head + 1]
        row = cumlog[head : head + 1, :]
        total = row[:, length - 1 : length]
        scores = dot_f32(query, key, ((1,), (1,))) * scaling
        weights = jnp.where(causal, jnp.exp(jnp.where(causal, column - row, 0.0)), 0.0)
        decayed = (scores * weights).astype(jnp.bfloat16)
        inside_out[:, span] = dot_f32(decayed, value, ((1,), (0,)))
        weighted = key.astype(jnp.float32) * jnp.exp(total - column)
        hi, lo = split_hi_lo(weighted)
        state = dot_f32(hi, value, ((0,), (0,))) + dot_f32(lo, value, ((0,), (0,)))
        state_out[head] = state
        message_out[head, 0:head_dim, :] = state.astype(jnp.bfloat16)
        wide = jnp.broadcast_to(total, (LOG_ROWS, head_dim))
        first, rest = split_hi_lo(wide)
        left = wide - first.astype(jnp.float32) - rest.astype(jnp.float32)
        pieces = jnp.where(
            row_at == 0,
            first.astype(jnp.float32),
            jnp.where(row_at == 1, rest.astype(jnp.float32), jnp.where(row_at == 2, left, 0.0)),
        )
        if head == 0:
            for choice in range(2):
                for chunk in range(length // head_dim):
                    piece = laid_out[
                        ROUTE_ROW + choice : ROUTE_ROW + choice + 1,
                        chunk * head_dim : (chunk + 1) * head_dim,
                    ]
                    at = 4 + choice * (length // head_dim) + chunk
                    pieces = jnp.where(row_at == at, piece, pieces)
        message_out[head, head_dim : head_dim + LOG_ROWS, :] = pieces.astype(jnp.bfloat16)


def finish_kernel(place_ref, *refs, planes, heads, head_dim):
    arrived = refs[: planes - 1]
    q_ref, inside_ref, cum_ref, own_ref, state_in_ref, gain_ref = refs[planes - 1 : planes + 5]
    outs = refs[planes + 5 :]
    x_outs, final_out = outs[:COLUMN_PARTS], outs[-1]
    plane = place_ref[2]
    a_part = heads // COLUMN_PARTS
    length = q_ref.shape[0]
    scaling = 1.0 / math.sqrt(head_dim)
    squares = jnp.zeros((length, head_dim), jnp.float32)

    def log_of(at, head):
        pieces = arrived[at][head, head_dim : head_dim + LOG_ROWS, :].astype(jnp.float32)
        return pieces[0:1] + pieces[1:2] + pieces[2:3]

    for head in range(heads):
        part, inner = head // a_part, head % a_part
        span = slice(head * head_dim, (head + 1) * head_dim)
        logs = [log_of(at, head) for at in range(planes - 1)]
        states = [arrived[at][head, 0:head_dim, :].astype(jnp.float32) for at in range(planes - 1)]
        passed = jnp.zeros((1, head_dim), jnp.float32)
        entering = jnp.zeros((head_dim, head_dim), jnp.float32)
        for at in range(planes - 1):
            earlier = at + 1 <= plane
            entering = entering + jnp.where(earlier, jnp.exp(passed), 0.0) * states[at]
            passed = passed + jnp.where(earlier, logs[at], 0.0)
        entering = entering + jnp.exp(passed) * state_in_ref[part, 0, inner]
        column = cum_ref[:, head : head + 1]
        own_log = cum_ref[length - 1 : length, head : head + 1]
        running = jnp.exp(own_log) * entering + own_ref[head]
        for at in reversed(range(planes - 1)):
            later = at + 1 > plane
            running = jnp.where(later, jnp.exp(logs[at]), 1.0) * running + jnp.where(
                later, states[at], 0.0
            )
        final_out[head] = running
        hi, lo = split_hi_lo(entering)
        query = q_ref[:, span]
        carried = dot_f32(query, hi, ((1,), (0,))) + dot_f32(query, lo, ((1,), (0,)))
        attended = (inside_ref[:, span] + carried * (jnp.exp(column) * scaling)).astype(
            jnp.bfloat16
        )
        wide = attended.astype(jnp.float32)
        squares = squares + wide * wide
        here = slice(inner * head_dim, (inner + 1) * head_dim)
        x_outs[part][0:length, here] = (wide * gain_ref[0, part, 0, :, here]).astype(jnp.bfloat16)
    sums = jnp.sum(squares, axis=1, keepdims=True)
    row = jnp.broadcast_to(jnp.broadcast_to(sums, (length, head_dim)).T[0:1, :], (LOG_ROWS, length))
    first, rest = split_hi_lo(row)
    first, rest = first.astype(jnp.float32), rest.astype(jnp.float32)
    row_at = lax.broadcasted_iota(jnp.int32, (LOG_ROWS, length), 0)
    left = jnp.where(row_at == 2, row - first - rest, 0.0)
    pieces = jnp.where(row_at == 0, first, jnp.where(row_at == 1, rest, left))
    x_outs[0][length : length + LOG_ROWS, :] = pieces.astype(jnp.bfloat16)


def select_kernel(place_ref, *refs, planes, group, experts, block, length):
    arrived, select_ref, target_ref = refs[:planes], refs[planes], refs[planes + 1]
    exp_at, plane = place_ref[1], place_ref[2]
    chunks = length // arrived[0].shape[2]
    a_select = BLOCKS_A_GROUP // group
    padded = target_ref.shape[1]
    expert_id = lax.broadcasted_iota(jnp.int32, (padded, length), 0) + exp_at * experts
    token = lax.broadcasted_iota(jnp.int32, (padded, length), 1)
    before = lax.broadcasted_iota(jnp.int32, (length, length), 0)
    after = lax.broadcasted_iota(jnp.int32, (length, length), 1)
    counting = ((before <= after) & (before // block == after // block)).astype(jnp.bfloat16)
    for shift in range(planes):
        source = lax.rem(plane - shift + planes, planes)
        pieces = arrived[shift][0].astype(jnp.float32)
        chosen = None
        for choice in range(2):
            named = jnp.concatenate(
                [
                    pieces[4 + choice * chunks + c : 5 + choice * chunks + c]
                    for c in range(chunks)
                ],
                axis=1,
            )
            hit = named.astype(jnp.int32) == expert_id
            chosen = hit if chosen is None else chosen | hit
        count = dot_f32(
            chosen.astype(jnp.float32).astype(jnp.bfloat16), counting, ((1,), (0,))
        ).astype(jnp.int32)
        in_select = lax.rem(source, a_select) * group + token // block
        target_ref[source] = jnp.where(chosen, in_select * CAP + count - 1, -1)
    slots = BLOCKS_A_GROUP * CAP
    slot = lax.broadcasted_iota(jnp.int32, (slots, a_select * length), 0)
    for at in range(planes // a_select):
        target = jnp.concatenate(
            [target_ref[at * a_select + i] for i in range(a_select)], axis=1
        )
        for expert in range(experts):
            select_ref[at, expert * slots : (expert + 1) * slots, :] = (
                (target[expert : expert + 1] == slot).astype(jnp.float32).astype(jnp.bfloat16)
            )


def expert_kernel(place_ref, x_ref, select_ref, gate_ref, up_ref, *refs, part, first, last):
    refs = list(refs)
    acc_in = None if first else refs.pop(0)
    scale_ref = refs.pop(0) if last else None
    out, rows_scratch, weights, acc, sems = refs
    expert, half = pl.program_id(0), pl.program_id(1)
    experts, halves = pl.num_programs(0), pl.num_programs(1)
    n_experts = rows_scratch.shape[0]
    group = x_ref.shape[1]
    length, columns = x_ref.shape[3], x_ref.shape[4]
    n_select, select_rows, select_tokens = select_ref.shape
    a_select = select_tokens // length
    slots = select_rows // n_experts
    hidden = gate_ref.shape[1]
    padded, depth = weights.shape[1] // 2, weights.shape[2]
    step = expert * halves + half
    slot = lax.rem(step, 2)

    def copies(step, slot):
        of_expert, of_half = step // halves, lax.rem(step, halves)
        block = jnp.bitwise_xor(of_half, place_ref[1]) * COLUMN_PARTS + part
        span = pl.ds(pl.multiple_of(block * depth, depth), depth)
        return [
            pltpu.make_async_copy(
                ref.at[of_expert, :, span],
                weights.at[slot, at * padded : at * padded + hidden],
                sems.at[slot, at],
            )
            for at, ref in enumerate((gate_ref, up_ref))
        ]

    @pl.when(step == 0)
    def _():
        for copy in copies(step, slot):
            copy.start()
        if padded > hidden:
            empty = jnp.zeros((2, padded - hidden, depth), jnp.bfloat16)
            weights[:, hidden:padded] = empty
            weights[:, padded + hidden : 2 * padded] = empty

    @pl.when(step + 1 < experts * halves)
    def _():
        for copy in copies(step + 1, 1 - slot):
            copy.start()

    @pl.when(expert == 0)
    def _():
        for at in range(n_select):
            for member in range(group):
                tokens = x_ref[at * a_select : (at + 1) * a_select, member, 0].reshape(
                    select_tokens, columns
                )
                picked = dot_f32(select_ref[at], tokens, ((1,), (0,))).astype(jnp.bfloat16)
                for e in range(n_experts):
                    rows_scratch[
                        e,
                        half,
                        at * slots : (at + 1) * slots,
                        member * columns : (member + 1) * columns,
                    ] = picked[e * slots : (e + 1) * slots]

    for copy in copies(step, slot):
        copy.wait()
    sums = dot_f32(rows_scratch[expert, half], weights[slot], ((1,), (1,)))

    @pl.when(half == 0)
    def _():
        acc[...] = sums if first else acc_in[0] + sums

    @pl.when(half > 0)
    def _():
        acc[...] += sums

    @pl.when(half == halves - 1)
    def _():
        if last:
            scale = scale_ref[0]
            gate = acc[:, 0:hidden] * scale
            up = acc[:, padded : padded + hidden] * scale
            out[0] = (gate / (1.0 + jnp.exp(-gate)) * up).astype(jnp.bfloat16)
        else:
            out[0] = acc[...]


def vmem_spec():
    return pl.BlockSpec(memory_space=pltpu.VMEM)


def smem_spec():
    return pl.BlockSpec(memory_space=pltpu.SMEM)


def expert_part(part, place, x, select, w_gate, w_up, acc, scale):
    first, last = acc is None, scale is not None
    experts, hidden, width = w_gate.shape
    planes, group, halves, _, columns = x.shape
    length = select.shape[2] * select.shape[0] // planes
    depth = group * columns
    n_rows = select.shape[0] * select.shape[1] // experts
    padded = -(-hidden // 128) * 128
    acc_spec = pl.BlockSpec((1, n_rows, 2 * padded), lambda e, half: (e, 0, 0))
    anywhere = pl.BlockSpec(memory_space=pl.ANY)
    in_specs = [
        smem_spec(),
        pl.BlockSpec(
            (planes, group, 1, length, columns),
            lambda e, half: (0, 0, jnp.where(e == 0, half, halves - 1), 0, 0),
        ),
        pl.BlockSpec(select.shape, lambda e, half: (0, 0, 0)),
        anywhere,
        anywhere,
    ]
    operands = [place, x, select, w_gate, w_up]
    aliases = {}
    if not first:
        in_specs.append(acc_spec)
        operands.append(acc)
    if last:
        in_specs.append(pl.BlockSpec((1, n_rows, 1), lambda e, half: (e, 0, 0)))
        operands.append(scale)
        out_shape = jax.ShapeDtypeStruct((experts, n_rows, hidden), jnp.bfloat16)
        out_spec = pl.BlockSpec((1, n_rows, hidden), lambda e, half: (e, 0, 0))
    else:
        out_shape = jax.ShapeDtypeStruct((experts, n_rows, 2 * padded), jnp.float32)
        out_spec = acc_spec
        if not first:
            aliases = {5: 0}
    return pl.pallas_call(
        functools.partial(expert_kernel, part=part, first=first, last=last),
        grid=(experts, halves),
        in_specs=in_specs,
        out_specs=out_spec,
        out_shape=out_shape,
        input_output_aliases=aliases,
        scratch_shapes=[
            pltpu.VMEM((experts, halves, n_rows, depth), jnp.bfloat16),
            pltpu.VMEM((2, 2 * padded, depth), jnp.bfloat16),
            pltpu.VMEM((n_rows, 2 * padded), jnp.float32),
            pltpu.SemaphoreType.DMA((2, 2)),
        ],
        compiler_params=pltpu.CompilerParams(vmem_limit_bytes=56 * MIB),
        cost_estimate=pl.CostEstimate(
            flops=4 * experts * hidden * n_rows * depth * halves,
            bytes_accessed=4 * experts * hidden * depth * halves,
            transcendentals=0,
        ),
        name="expert_part",
    )(*operands)


def shards(queries, keys, values, log_decay, state_in, norm_gain, routes, w_gate, w_up, *, shape):
    n_seq, n_exp = shape["seq"], shape["exp"]
    block, features = queries.shape
    local_heads, head_dim = state_in.shape[0], state_in.shape[1]
    group = next(
        g for g in (4, 2, 1) if local_heads % (g * COLUMN_PARTS) == 0 and n_seq % g == 0
    )
    planes = n_seq // group
    heads = local_heads // group
    a_part = heads // COLUMN_PARTS
    columns = a_part * head_dim
    length = group * block
    width = heads * head_dim
    seq_at = lax.axis_index("seq")
    exp_at = lax.axis_index("exp")
    member_at = seq_at % group
    plane_at = seq_at // group
    place = jnp.stack([member_at, exp_at, plane_at]).astype(jnp.int32)

    def to_member(a, hop):
        if hop == 0:
            return a
        pairs = [(s, s // group * group + ((s % group) ^ hop)) for s in range(n_seq)]
        return lax.ppermute(a, "seq", pairs)

    def to_plane(a, shift):
        pairs = [((s), (s // group + shift) % planes * group + s % group) for s in range(n_seq)]
        return lax.ppermute(a, "seq", pairs)

    by_member = log_decay.reshape(COLUMN_PARTS, group, a_part, block).transpose(1, 0, 2, 3)
    by_member = by_member.reshape(group, heads, block)
    by_member = jnp.pad(by_member, ((0, 0), (0, ROUTE_ROW - heads), (0, 0)))
    named = jnp.broadcast_to(routes.T.astype(jnp.float32)[None], (group, 2, block))
    by_member = jnp.concatenate([by_member, named], axis=1)
    smem = smem_spec()
    packed = pl.pallas_call(
        functools.partial(pack_kernel, group=group, columns=columns),
        in_specs=[smem] + [vmem_spec()] * 4,
        out_specs=[vmem_spec()] * (2 * group),
        out_shape=[jax.ShapeDtypeStruct((3 * block, width), jnp.bfloat16)] * group
        + [jax.ShapeDtypeStruct((8, block), jnp.float32)] * group,
        compiler_params=pltpu.CompilerParams(vmem_limit_bytes=16 * MIB),
        name="pack",
    )(place, queries, keys, values, by_member)
    messages = [to_member(packed[hop], hop) for hop in range(group)]
    logs = [to_member(packed[group + hop], hop) for hop in range(group)]

    query, inside, cumlog, own_state, message = pl.pallas_call(
        functools.partial(
            local_kernel, group=group, heads=heads, head_dim=head_dim, block=block
        ),
        in_specs=[smem] + [vmem_spec()] * (2 * group),
        out_specs=[vmem_spec()] * 5,
        out_shape=[
            jax.ShapeDtypeStruct((length, width), jnp.bfloat16),
            jax.ShapeDtypeStruct((length, width), jnp.float32),
            jax.ShapeDtypeStruct((length, 8), jnp.float32),
            jax.ShapeDtypeStruct((heads, head_dim, head_dim), jnp.float32),
            jax.ShapeDtypeStruct((heads, head_dim + LOG_ROWS, head_dim), jnp.bfloat16),
        ],
        scratch_shapes=[
            pltpu.VMEM((length, width), jnp.bfloat16),
            pltpu.VMEM((length, width), jnp.bfloat16),
            pltpu.VMEM((group, 8, block), jnp.float32),
        ],
        compiler_params=pltpu.CompilerParams(vmem_limit_bytes=24 * MIB),
        name="local_attention",
    )(place, *messages, *logs)
    arrived = [to_plane(message, shift) for shift in range(1, planes)]

    experts = w_gate.shape[0]
    slots = BLOCKS_A_GROUP * CAP
    n_select = n_seq // BLOCKS_A_GROUP
    routes_spec = pl.BlockSpec(
        (1, LOG_ROWS, head_dim), lambda i, place: (0, head_dim // LOG_ROWS, 0)
    )
    select = pl.pallas_call(
        functools.partial(
            select_kernel,
            planes=planes,
            group=group,
            experts=experts,
            block=block,
            length=length,
        ),
        grid_spec=pltpu.PrefetchScalarGridSpec(
            num_scalar_prefetch=1,
            grid=(1,),
            in_specs=[routes_spec] * planes,
            out_specs=pl.BlockSpec(
                (n_select, experts * slots, BLOCKS_A_GROUP * block), lambda i, place: (0, 0, 0)
            ),
            scratch_shapes=[pltpu.VMEM((planes, 8, length), jnp.int32)],
        ),
        out_shape=jax.ShapeDtypeStruct(
            (n_select, experts * slots, BLOCKS_A_GROUP * block), jnp.bfloat16
        ),
        compiler_params=pltpu.CompilerParams(vmem_limit_bytes=16 * MIB),
        name="select_rows",
    )(place, message, *arrived)

    part_rows = [length + LOG_ROWS] + [length] * (COLUMN_PARTS - 1)
    whole = lambda *dims: pl.BlockSpec(dims, lambda i, place: (0,) * len(dims))
    state_blocks = state_in.reshape(COLUMN_PARTS, group, a_part, head_dim, head_dim)
    gain_blocks = norm_gain.reshape(n_exp, COLUMN_PARTS, group, 1, columns)
    finished = pl.pallas_call(
        functools.partial(finish_kernel, planes=planes, heads=heads, head_dim=head_dim),
        grid_spec=pltpu.PrefetchScalarGridSpec(
            num_scalar_prefetch=1,
            grid=(1,),
            in_specs=[whole(heads, head_dim + LOG_ROWS, head_dim)] * (planes - 1)
            + [
                whole(length, width),
                whole(length, width),
                whole(length, 8),
                whole(heads, head_dim, head_dim),
                pl.BlockSpec(
                    (COLUMN_PARTS, 1, a_part, head_dim, head_dim),
                    lambda i, place: (0, place[0], 0, 0, 0),
                ),
                pl.BlockSpec(
                    (1, COLUMN_PARTS, 1, 1, columns),
                    lambda i, place: (place[1], 0, place[0], 0, 0),
                ),
            ],
            out_specs=[whole(n_tokens, columns) for n_tokens in part_rows]
            + [whole(heads, head_dim, head_dim)],
        ),
        out_shape=[
            jax.ShapeDtypeStruct((n_tokens, columns), jnp.bfloat16) for n_tokens in part_rows
        ]
        + [jax.ShapeDtypeStruct((heads, head_dim, head_dim), jnp.float32)],
        compiler_params=pltpu.CompilerParams(vmem_limit_bytes=32 * MIB),
        name="finish_attention",
    )(place, *arrived, query, inside, cumlog, own_state, state_blocks, gain_blocks)
    x_parts, final = finished[:COLUMN_PARTS], finished[-1]

    def to_half(a, hop):
        if hop == 0:
            return a
        return lax.ppermute(a, "exp", [(e, e ^ hop) for e in range(n_exp)])

    gathered = []
    for x in x_parts:
        halves = jnp.stack([to_half(x, hop) for hop in range(n_exp)])
        gathered.append(
            lax.all_gather(halves, "seq").reshape(planes, group, n_exp, x.shape[0], columns)
        )
    pieces = gathered[0][:, :, :, length : length + 3, :].astype(jnp.float32)
    mean = jnp.sum(pieces, axis=(1, 2, 3)) / (n_exp * features)
    token_scale = lax.rsqrt(mean + EPSILON).reshape(n_select, 1, BLOCKS_A_GROUP * block)
    slot_scale = jnp.sum(select.astype(jnp.float32) * token_scale, axis=2)
    slot_scale = slot_scale.reshape(n_select, experts, slots).transpose(1, 0, 2)
    slot_scale = slot_scale.reshape(experts, n_select * slots, 1)

    acc = None
    for part in range(COLUMN_PARTS):
        scale = slot_scale if part == COLUMN_PARTS - 1 else None
        acc = expert_part(part, place, gathered[part], select, w_gate, w_up, acc, scale)
    hidden = acc.swapaxes(1, 2)

    out_rows = head_dim // n_seq
    pieces = []
    for hop in range(group):
        dest = plane_at * group + jnp.bitwise_xor(member_at, hop)
        piece = lax.dynamic_slice_in_dim(final, dest * out_rows, out_rows, 1)
        pieces.append(to_member(piece, hop))
    stacked = jnp.stack(pieces)
    ordered = [
        lax.dynamic_index_in_dim(stacked, jnp.bitwise_xor(member_at, m), 0, False)
        for m in range(group)
    ]
    ordered = [a.reshape(COLUMN_PARTS, a_part, out_rows, head_dim) for a in ordered]
    state_out = jnp.stack(ordered, axis=1).reshape(local_heads, out_rows, head_dim)
    return (hidden, state_out)


def solution(mesh):
    placed = (
        P("seq", "exp"),
        P("seq", "exp"),
        P("seq", "exp"),
        P("exp", "seq"),
        P("exp", None, None),
        P(),
        P("seq", None),
        P("exp", "seq", None),
        P("exp", "seq", None),
    )
    return jax.shard_map(
        functools.partial(shards, shape=dict(mesh.shape)),
        mesh=mesh,
        in_specs=placed,
        out_specs=(P("exp", "seq", None), P("exp", "seq", None)),
        check_vma=False,
    )
```

```python
import functools
import math

import jax
import jax.numpy as jnp
from jax import lax
from jax.experimental import pallas as pl
from jax.experimental.pallas import tpu as pltpu
from jax.sharding import PartitionSpec as P

CAP = 20
EPSILON = 1e-06
LANES = 128
BLOCKS_A_PLANE = 4
WEIGHT_PIECES = 2
LOG_ROWS = 16
ROUTE_ROW = 6
MIB = 1 << 20


def split_hi_lo(wide):
    hi = wide.astype(jnp.bfloat16)
    return hi, (wide - hi.astype(jnp.float32)).astype(jnp.bfloat16)


def dot_f32(a, b, dims, precision=None):
    return lax.dot_general(
        a, b, (dims, ((), ())), precision=precision, preferred_element_type=jnp.float32
    )


def position(group):
    at = lax.axis_index("seq")
    return lax.rem(at, group), lax.axis_index("exp"), lax.div(at, group)


def pack_kernel(
    q_ref, k_ref, v_ref, state_ref, gain_ref, log_ref, named_ref, *refs, group
):
    outs, state_out, gain_out, sems = refs[: 2 * group], *refs[2 * group :]
    block = q_ref.shape[0]
    width = q_ref.shape[1] // group
    heads = log_ref.shape[0] // group
    mine, half, _ = position(group)
    copies = []
    for hop in range(group):
        dest = jnp.bitwise_xor(mine, hop)
        source = pl.ds(pl.multiple_of(dest * width, width), width)
        for at, ref in enumerate((q_ref, k_ref, v_ref)):
            copies.append(
                pltpu.make_async_copy(
                    ref.at[:, source],
                    outs[hop].at[at * block : (at + 1) * block],
                    sems.at[hop, at],
                )
            )
    gain_at = (half * group + mine) * width
    copies.append(
        pltpu.make_async_copy(
            gain_ref.at[:, pl.ds(pl.multiple_of(gain_at, width), width)], gain_out, sems.at[group, 0]
        )
    )
    copies.append(
        pltpu.make_async_copy(
            state_ref.at[pl.ds(mine * heads, heads)], state_out, sems.at[group, 1]
        )
    )
    for copy in copies:
        copy.start()
    for hop in range(group):
        logs = outs[group + hop]
        logs[...] = jnp.zeros_like(logs)
        logs[0:heads, :] = log_ref[pl.ds(jnp.bitwise_xor(mine, hop) * heads, heads), :]
        logs[ROUTE_ROW : ROUTE_ROW + 2, :] = named_ref[...].astype(jnp.float32)
    for copy in copies:
        copy.wait()


def local_kernel(*refs, group, heads, head_dim, block):
    messages, logs = refs[:group], refs[group : 2 * group]
    q_out, inside_out, cum_out, state_out, message_out = refs[2 * group : 2 * group + 5]
    k_all, v_all, log_all = refs[2 * group + 5 :]
    mine, _, _ = position(group)
    length = group * block
    for hop in range(group):
        source = jnp.bitwise_xor(mine, hop)
        rows = pl.ds(pl.multiple_of(source * block, block), block)
        q_out[rows, :] = messages[hop][0:block, :]
        k_all[rows, :] = messages[hop][block : 2 * block, :]
        v_all[rows, :] = messages[hop][2 * block : 3 * block, :]
        log_all[source] = logs[hop][...]
    cumlog = jnp.zeros((log_all.shape[1], length), jnp.float32)
    laid_out = jnp.zeros((log_all.shape[1], length), jnp.float32)
    for at in range(group):
        before = lax.broadcasted_iota(jnp.int32, (block, length), 0) + at * block
        after = lax.broadcasted_iota(jnp.int32, (block, length), 1)
        cumlog = cumlog + dot_f32(
            log_all[at],
            (before <= after).astype(jnp.float32),
            ((1,), (0,)),
            lax.Precision.HIGHEST,
        )
        laid_out = laid_out + dot_f32(
            log_all[at],
            (before == after).astype(jnp.float32),
            ((1,), (0,)),
            lax.Precision.HIGHEST,
        )
    cum_columns = cumlog.T
    cum_out[...] = cum_columns
    scaling = 1.0 / math.sqrt(head_dim)
    causal = lax.broadcasted_iota(jnp.int32, (length, length), 0) >= lax.broadcasted_iota(
        jnp.int32, (length, length), 1
    )
    row_at = lax.broadcasted_iota(jnp.int32, (LOG_ROWS, head_dim), 0)
    for head in range(heads):
        span = slice(head * head_dim, (head + 1) * head_dim)
        query, key, value = q_out[:, span], k_all[:, span], v_all[:, span]
        column = cum_columns[:, head : head + 1]
        row = cumlog[head : head + 1, :]
        total = row[:, length - 1 : length]
        scores = dot_f32(query, key, ((1,), (1,))) * scaling
        weights = jnp.where(causal, jnp.exp(jnp.where(causal, column - row, 0.0)), 0.0)
        decayed = (scores * weights).astype(jnp.bfloat16)
        inside_out[:, span] = dot_f32(decayed, value, ((1,), (0,)))
        weighted = key.astype(jnp.float32) * jnp.exp(total - column)
        hi, lo = split_hi_lo(weighted)
        state = dot_f32(hi, value, ((0,), (0,))) + dot_f32(lo, value, ((0,), (0,)))
        state_out[head] = state
        message_out[head, 0:head_dim, :] = state.astype(jnp.bfloat16)
        wide = jnp.broadcast_to(total, (LOG_ROWS, head_dim))
        first, rest = split_hi_lo(wide)
        left = wide - first.astype(jnp.float32) - rest.astype(jnp.float32)
        pieces = jnp.where(
            row_at == 0,
            first.astype(jnp.float32),
            jnp.where(row_at == 1, rest.astype(jnp.float32), jnp.where(row_at == 2, left, 0.0)),
        )
        if head == 0:
            for choice in range(2):
                for chunk in range(length // head_dim):
                    piece = laid_out[
                        ROUTE_ROW + choice : ROUTE_ROW + choice + 1,
                        chunk * head_dim : (chunk + 1) * head_dim,
                    ]
                    at = 4 + choice * (length // head_dim) + chunk
                    pieces = jnp.where(row_at == at, piece, pieces)
        message_out[head, head_dim : head_dim + LOG_ROWS, :] = pieces.astype(jnp.bfloat16)


def finish_kernel(*refs, planes, group, heads, head_dim):
    arrived = refs[: planes - 1]
    q_ref, inside_ref, cum_ref, own_ref, state_in_ref, gain_ref = refs[planes - 1 : planes + 5]
    x_out, *piece_outs = refs[planes + 5 : planes + 6 + group]
    final = refs[planes + 6 + group]
    mine, _, plane = position(group)
    length, width = q_ref.shape
    scaling = 1.0 / math.sqrt(head_dim)
    squares = jnp.zeros((length, head_dim), jnp.float32)

    def log_of(at, head):
        pieces = arrived[at][head, head_dim : head_dim + LOG_ROWS, :].astype(jnp.float32)
        return pieces[0:1] + pieces[1:2] + pieces[2:3]

    for head in range(heads):
        span = slice(head * head_dim, (head + 1) * head_dim)
        logs = [log_of(at, head) for at in range(planes - 1)]
        states = [arrived[at][head, 0:head_dim, :].astype(jnp.float32) for at in range(planes - 1)]
        passed = jnp.zeros((1, head_dim), jnp.float32)
        entering = jnp.zeros((head_dim, head_dim), jnp.float32)
        for at in range(planes - 1):
            earlier = at + 1 <= plane
            entering = entering + jnp.where(earlier, jnp.exp(passed), 0.0) * states[at]
            passed = passed + jnp.where(earlier, logs[at], 0.0)
        entering = entering + jnp.exp(passed) * state_in_ref[head]
        column = cum_ref[:, head : head + 1]
        own_log = cum_ref[length - 1 : length, head : head + 1]
        running = jnp.exp(own_log) * entering + own_ref[head]
        for at in reversed(range(planes - 1)):
            later = at + 1 > plane
            running = jnp.where(later, jnp.exp(logs[at]), 1.0) * running + jnp.where(
                later, states[at], 0.0
            )
        final[...] = running
        for hop, piece in enumerate(piece_outs):
            n_rows = piece.shape[1]
            member = jnp.bitwise_xor(mine, hop)
            piece[head] = final[pl.ds((plane * group + member) * n_rows, n_rows), :]
        hi, lo = split_hi_lo(entering)
        query = q_ref[:, span]
        carried = dot_f32(query, hi, ((1,), (0,))) + dot_f32(query, lo, ((1,), (0,)))
        attended = (inside_ref[:, span] + carried * (jnp.exp(column) * scaling)).astype(
            jnp.bfloat16
        )
        wide = attended.astype(jnp.float32)
        squares = squares + wide * wide
        x_out[span, :] = (wide * gain_ref[:, span]).T.astype(jnp.bfloat16)
    sums = jnp.sum(squares, axis=1, keepdims=True)
    row = jnp.broadcast_to(sums, (length, head_dim)).T[0:LOG_ROWS, :]
    first, rest = split_hi_lo(row)
    first, rest = first.astype(jnp.float32), rest.astype(jnp.float32)
    row_at = lax.broadcasted_iota(jnp.int32, (LOG_ROWS, length), 0)
    left = jnp.where(row_at == 2, row - first - rest, 0.0)
    pieces = jnp.where(row_at == 0, first, jnp.where(row_at == 1, rest, left))
    x_out[width : width + LOG_ROWS, :] = pieces.astype(jnp.bfloat16)


def order_kernel(*refs, group, heads):
    mine, _, _ = position(group)
    pieces, out = refs[:group], refs[group]
    for hop in range(group):
        source = jnp.bitwise_xor(mine, hop)
        out[pl.ds(source * heads, heads)] = pieces[hop][...]


def select_kernel(*refs, group, planes, experts, block, length):
    arrived, target_ref, select_ref = refs[:planes], refs[planes], refs[planes + 1]
    _, exp_at, plane = position(group)
    chunks = length // LANES
    padded = target_ref.shape[1]
    expert_id = lax.broadcasted_iota(jnp.int32, (padded, length), 0) + exp_at * experts
    token = lax.broadcasted_iota(jnp.int32, (padded, length), 1)
    before = lax.broadcasted_iota(jnp.int32, (length, length), 0)
    after = lax.broadcasted_iota(jnp.int32, (length, length), 1)
    counting = ((before <= after) & (before // block == after // block)).astype(jnp.bfloat16)
    slot = lax.broadcasted_iota(jnp.int32, (length, LANES), 1)
    for shift in range(planes):
        source = lax.rem(plane - shift + planes, planes)
        pieces = arrived[shift][0].astype(jnp.float32)
        chosen = None
        for choice in range(2):
            named = jnp.concatenate(
                [
                    pieces[4 + choice * chunks + c : 5 + choice * chunks + c]
                    for c in range(chunks)
                ],
                axis=1,
            )
            hit = named.astype(jnp.int32) == expert_id
            chosen = hit if chosen is None else chosen | hit
        count = dot_f32(
            chosen.astype(jnp.float32).astype(jnp.bfloat16), counting, ((1,), (0,))
        ).astype(jnp.int32)
        target = jnp.where(chosen, token // block * CAP + count - 1, -1)
        target_ref[source] = target
        columns = target.astype(jnp.float32).T.astype(jnp.int32)
        for expert in range(experts):
            select_ref[source, :, expert * LANES : (expert + 1) * LANES] = (
                (columns[:, expert : expert + 1] == slot).astype(jnp.float32).astype(jnp.bfloat16)
            )


def spread_kernel(q_ref, k_ref, v_ref, log_ref, named_ref, *outs):
    block = q_ref.shape[0]
    mine = lax.axis_index("seq")
    row_at = lax.broadcasted_iota(jnp.int32, (LOG_ROWS, block), 0)
    named = named_ref[...].astype(jnp.float32)

    def extra(head):
        wide = log_ref[pl.ds(head, 1), :]
        first, rest = split_hi_lo(wide)
        first, rest = first.astype(jnp.float32), rest.astype(jnp.float32)
        tile = jnp.zeros((LOG_ROWS, block), jnp.float32)
        pieces = (first, rest, wide - first - rest, named[0:1], named[1:2])
        for at, piece in enumerate(pieces):
            tile = jnp.where(row_at == at, piece, tile)
        return tile.astype(jnp.bfloat16)

    for hop, out in enumerate(outs):
        dest = jnp.bitwise_xor(mine, hop)
        chip, core = lax.div(dest, 2), lax.rem(dest, 2)
        out[3 * block : 3 * block + LOG_ROWS, :] = jnp.zeros(
            (LOG_ROWS, out.shape[1]), jnp.bfloat16
        )
        for side, head in enumerate((3 * chip + 2 * core, 3 * chip + 1)):
            source = pl.ds(pl.multiple_of(head * LANES, LANES), LANES)
            target = slice(side * LANES, (side + 1) * LANES)
            for at, ref in enumerate((q_ref, k_ref, v_ref)):
                out[at * block : (at + 1) * block, target] = ref[:, source]
            out[3 * block : 3 * block + LOG_ROWS, side * LANES : side * LANES + block] = extra(head)


def attend_kernel(*refs, block, chunk):
    hops = len(refs) - 12
    messages = refs[:hops]
    state_ref, gain_ref, x_out, final_out, named_out = refs[hops : hops + 5]
    every, state, gain, shared, state_sem, gain_sem, running = refs[hops + 5 :]
    mine = lax.axis_index("seq")
    chip, core = lax.div(mine, 2), lax.rem(mine, 2)
    width = gain.shape[1]
    gain_at = lax.axis_index("exp") * (hops // 2 * width) + chip * width
    copies = [
        pltpu.make_async_copy(state_ref.at[pl.ds(3 * chip, 3)], state, state_sem),
        pltpu.make_async_copy(
            gain_ref.at[:, pl.ds(pl.multiple_of(gain_at, LANES), width)], gain, gain_sem
        ),
    ]
    for copy in copies:
        copy.start()
    for hop, message in enumerate(messages):
        every[jnp.bitwise_xor(mine, hop)] = message[...]
    scaling = 1.0 / math.sqrt(LANES)
    causal = lax.broadcasted_iota(jnp.int32, (chunk, chunk), 0) >= lax.broadcasted_iota(
        jnp.int32, (chunk, chunk), 1
    )
    lane = lax.broadcasted_iota(jnp.int32, (chunk, LANES), 1)
    half_mask = lax.div(lane, LANES // 2) == core
    row_at = lax.broadcasted_iota(jnp.int32, (LOG_ROWS, chunk), 0)
    before = lax.broadcasted_iota(jnp.int32, (block, chunk), 0)
    after = lax.broadcasted_iota(jnp.int32, (block, chunk), 1)
    a_chunk = chunk // block
    own_rows = x_out.shape[0] - LOG_ROWS
    for copy in copies:
        copy.wait()
    running[0] = state[2 * core]
    running[1] = state[1]
    gain_own = gain[:, pl.ds(pl.multiple_of(2 * core * LANES, LANES), LANES)]
    gains = (gain_own, gain[:, LANES : 2 * LANES])
    for part in range(hops // a_chunk):
        tokens = slice(part * chunk, (part + 1) * chunk)
        cumlog = jnp.zeros((8, chunk), jnp.float32)
        named = jnp.zeros((8, chunk), jnp.float32)
        for at in range(a_chunk):
            pieces = every[part * a_chunk + at, 3 * block : 3 * block + LOG_ROWS, :].astype(
                jnp.float32
            )
            logs = pieces[0:1] + pieces[1:2] + pieces[2:3]
            rows = jnp.concatenate(
                [
                    logs[:, 0:block],
                    logs[:, LANES : LANES + block],
                    pieces[3:5, 0:block],
                    jnp.zeros((4, block), jnp.float32),
                ],
                axis=0,
            )
            cumlog = cumlog + dot_f32(
                rows,
                (before + at * block <= after).astype(jnp.float32),
                ((1,), (0,)),
                lax.Precision.HIGHEST,
            )
            named = named + dot_f32(
                rows, (before + at * block == after).astype(jnp.float32), ((1,), (0,))
            )
        named_out[:, tokens] = named
        columns = cumlog.T
        squares = None
        for side in range(2):
            span = slice(side * LANES, (side + 1) * LANES)

            def whole_chunk(at):
                some = every[
                    part * a_chunk : (part + 1) * a_chunk, at * block : (at + 1) * block, span
                ]
                return some.reshape(chunk, LANES)

            query, key, value = whole_chunk(0), whole_chunk(1), whole_chunk(2)
            column, row = columns[:, side : side + 1], cumlog[side : side + 1, :]
            total = row[:, chunk - 1 : chunk]
            scores = dot_f32(query, key, ((1,), (1,))) * scaling
            weights = jnp.where(causal, jnp.exp(jnp.where(causal, column - row, 0.0)), 0.0)
            decayed = (scores * weights).astype(jnp.bfloat16)
            inside = dot_f32(decayed, value, ((1,), (0,)))
            entering = running[side]
            hi, lo = split_hi_lo(entering)
            carried = dot_f32(query, hi, ((1,), (0,))) + dot_f32(query, lo, ((1,), (0,)))
            attended = (inside + carried * (jnp.exp(column) * scaling)).astype(jnp.bfloat16)
            hi, lo = split_hi_lo(key.astype(jnp.float32) * jnp.exp(total - column))
            added = dot_f32(hi, value, ((0,), (0,))) + dot_f32(lo, value, ((0,), (0,)))
            running[side] = jnp.exp(total) * entering + added
            wide = attended.astype(jnp.float32)
            turned = (wide * gains[side]).T.astype(jnp.bfloat16)
            if side == 0:
                squares = wide * wide
                at = pl.multiple_of(core * (LANES // 2), LANES // 2)
                x_out[pl.ds(at, LANES), tokens] = turned
            else:
                squares = squares + jnp.where(half_mask, wide * wide, 0.0)
                shared[...] = turned
                at = pl.multiple_of((1 - core) * LANES, LANES // 2)
                taken = pl.multiple_of(core * (LANES // 2), LANES // 2)
                x_out[pl.ds(at, LANES // 2), tokens] = shared[pl.ds(taken, LANES // 2), :]
        sums = jnp.sum(squares, axis=1, keepdims=True)
        row = jnp.broadcast_to(sums, (chunk, LANES)).T[0:LOG_ROWS, :]
        first, rest = split_hi_lo(row)
        first, rest = first.astype(jnp.float32), rest.astype(jnp.float32)
        left = jnp.where(row_at == 2, row - first - rest, 0.0)
        pieces = jnp.where(row_at == 0, first, jnp.where(row_at == 1, rest, left))
        x_out[own_rows : own_rows + LOG_ROWS, tokens] = pieces.astype(jnp.bfloat16)
    final_out[:, 0:LANES] = running[0]
    final_out[:, LANES : 2 * LANES] = jnp.where(half_mask[0:LANES], running[1], 0.0)


def choose_kernel(named_ref, select_ref, *, experts, block):
    chunk = select_ref.shape[1]
    exp_at = lax.axis_index("exp")
    expert_id = lax.broadcasted_iota(jnp.int32, (8, chunk), 0) + exp_at * experts
    token = lax.broadcasted_iota(jnp.int32, (8, chunk), 1)
    before = lax.broadcasted_iota(jnp.int32, (chunk, chunk), 0)
    after = lax.broadcasted_iota(jnp.int32, (chunk, chunk), 1)
    counting = ((before <= after) & (before // block == after // block)).astype(jnp.bfloat16)
    slot = lax.broadcasted_iota(jnp.int32, (chunk, LANES), 1)
    for part in range(select_ref.shape[0]):
        named = named_ref[:, part * chunk : (part + 1) * chunk].astype(jnp.int32)
        chosen = (named[2:3] == expert_id) | (named[3:4] == expert_id)
        count = dot_f32(
            chosen.astype(jnp.float32).astype(jnp.bfloat16), counting, ((1,), (0,))
        ).astype(jnp.int32)
        target = jnp.where(chosen, token // block * CAP + count - 1, -1)
        columns = target.astype(jnp.float32).T.astype(jnp.int32)
        for expert in range(experts):
            select_ref[part, :, expert * LANES : (expert + 1) * LANES] = (
                (columns[:, expert : expert + 1] == slot).astype(jnp.float32).astype(jnp.bfloat16)
            )


def join_kernel(*refs):
    arrived, out = refs[0], refs[1]
    for chip in range(out.shape[0] // 3):
        low, high = arrived[2 * chip], arrived[2 * chip + 1]
        out[3 * chip] = low[:, 0:LANES]
        out[3 * chip + 1] = low[:, LANES:] + high[:, LANES:]
        out[3 * chip + 2] = high[:, 0:LANES]


def expert_kernel(*refs, hops, first, last, features):
    refs = list(refs)
    blocks = [(refs.pop(0), refs.pop(0)) for _ in hops]
    select_ref, gate_ref, up_ref = refs.pop(0), refs.pop(0), refs.pop(0)
    acc_in, sums_in = (None, None) if first else (refs.pop(0), refs.pop(0))
    out = refs.pop(0)
    sums_out = None if last else refs.pop(0)
    rows, weights, sems, tokens, extras, token_sems = [refs.pop(0) for _ in range(6)]
    experts, hidden = rows.shape[0], weights.shape[1] // 2
    slots_buffered = weights.shape[0]
    parts, chunk = select_ref.shape[0], select_ref.shape[1]
    own = blocks[0][0].shape[0] - LOG_ROWS
    depth = 2 * own
    mine, half = lax.axis_index("seq"), lax.axis_index("exp")
    chip, core = lax.div(mine, 2), lax.rem(mine, 2)
    piece = hidden // WEIGHT_PIECES

    def copies(expert):
        at = expert % slots_buffered
        found = []
        for c, (hop_chip, hop_half) in enumerate(hops):
            start = jnp.bitwise_xor(half, hop_half) * (features // 2)
            start = start + jnp.bitwise_xor(chip, hop_chip) * depth
            span = pl.ds(pl.multiple_of(start, LANES), depth)
            for i, ref in enumerate((gate_ref, up_ref)):
                for n in range(WEIGHT_PIECES):
                    found.append(
                        pltpu.make_async_copy(
                            ref.at[expert, n * piece : (n + 1) * piece, span],
                            weights.at[
                                at,
                                i * hidden + n * piece : i * hidden + (n + 1) * piece,
                                c * depth : (c + 1) * depth,
                            ],
                            sems.at[at, c, i, n],
                        )
                    )
        return found

    arrivals = []
    for c, pair in enumerate(blocks):
        for side, block in enumerate(pair):
            at = c * depth + jnp.bitwise_xor(core, side) * own
            arrivals.append(
                pltpu.make_async_copy(
                    block.at[0:own],
                    tokens.at[pl.ds(pl.multiple_of(at, own), own)],
                    token_sems.at[c, side, 0],
                )
            )
            arrivals.append(
                pltpu.make_async_copy(
                    block.at[own : own + LOG_ROWS], extras.at[c, side], token_sems.at[c, side, 1]
                )
            )
    for copy in arrivals:
        copy.start()
    for expert in range(min(slots_buffered - 1, experts)):
        for copy in copies(expert):
            copy.start()
    for copy in arrivals:
        copy.wait()
    for part in range(parts):
        picked = dot_f32(
            tokens[:, part * chunk : (part + 1) * chunk], select_ref[part], ((1,), (0,))
        ).astype(jnp.bfloat16)
        for e in range(experts):
            rows[e, :, part * LANES : (part + 1) * LANES] = picked[:, e * LANES : (e + 1) * LANES]
    pieces = jnp.zeros((LOG_ROWS, extras.shape[3]), jnp.float32)
    for c in range(len(hops)):
        for side in range(2):
            pieces = pieces + extras[c, side].astype(jnp.float32)
    total = pieces[0:1] + pieces[1:2] + pieces[2:3]
    if not first:
        total = total + sums_in[0:1, :]
    total = jnp.broadcast_to(total, (8, total.shape[1]))
    if not last:
        sums_out[...] = total
    else:
        out_rows, out_sems = refs
        used = out_rows.shape[1] // parts
        factor = lax.rsqrt(total / features + EPSILON)
        scales = [
            dot_f32(
                factor[:, part * chunk : (part + 1) * chunk],
                select_ref[part].astype(jnp.float32),
                ((1,), (0,)),
                lax.Precision.HIGHEST,
            )[0:1]
            for part in range(parts)
        ]
    for expert in range(experts):
        ahead = expert + slots_buffered - 1
        if ahead < experts:
            for copy in copies(ahead):
                copy.start()
        for copy in copies(expert):
            copy.wait()
        sums = dot_f32(weights[expert % slots_buffered], rows[expert], ((1,), (0,)))
        if not first:
            sums = acc_in[expert] + sums
        if not last:
            out[expert] = sums
            continue
        scale = jnp.concatenate(
            [one[:, expert * LANES : (expert + 1) * LANES] for one in scales], axis=1
        )
        gate = sums[0:hidden, :] * scale
        up = sums[hidden : 2 * hidden, :] * scale
        result = gate / (1.0 + jnp.exp(-gate)) * up
        wide = -(-hidden // LANES) * LANES
        if wide > hidden:
            result = jnp.concatenate(
                [result, jnp.zeros((wide - hidden, parts * LANES), jnp.float32)], axis=0
            )
        turned = result.T.astype(jnp.bfloat16)
        for part in range(parts):
            out_rows[expert, part * used : (part + 1) * used, :] = turned[
                part * LANES : part * LANES + used, 0:hidden
            ]
        pltpu.make_async_copy(out_rows.at[expert], out.at[expert], out_sems.at[expert]).start()
    if last:
        for expert in range(experts):
            pltpu.make_async_copy(out_rows.at[expert], out.at[expert], out_sems.at[expert]).wait()


def vmem_spec():
    return pl.BlockSpec(memory_space=pltpu.VMEM)


def expert_part(hops, blocks, select, w_gate, w_up, carry, last, features):
    first, parts = carry is None, select.shape[0]
    experts, ff, _ = w_gate.shape
    own, length = blocks[0].shape[0] - LOG_ROWS, blocks[0].shape[1]
    depth = 2 * own * len(hops)
    anywhere = pl.BlockSpec(memory_space=pl.ANY)
    in_specs = [anywhere] * len(blocks) + [vmem_spec(), anywhere, anywhere]
    operands = [*blocks, select, w_gate, w_up]
    aliases = {}
    if not first:
        if not last:
            aliases = {len(operands): 0, len(operands) + 1: 1}
        in_specs += [vmem_spec()] * 2
        operands += carry
    scratch = [
        pltpu.VMEM((experts, depth, parts * LANES), jnp.bfloat16),
        pltpu.VMEM((3, 2 * ff, depth), jnp.bfloat16),
        pltpu.SemaphoreType.DMA((3, len(hops), 2, WEIGHT_PIECES)),
        pltpu.VMEM((depth, length), jnp.bfloat16),
        pltpu.VMEM((len(hops), 2, LOG_ROWS, length), jnp.bfloat16),
        pltpu.SemaphoreType.DMA((len(hops), 2, 2)),
    ]
    if last:
        slots = parts * BLOCKS_A_PLANE * CAP
        scratch += [
            pltpu.VMEM((experts, slots, ff), jnp.bfloat16),
            pltpu.SemaphoreType.DMA((experts,)),
        ]
        out_shape = jax.ShapeDtypeStruct((experts, slots, ff), jnp.bfloat16)
        out_specs = anywhere
    else:
        out_shape = [
            jax.ShapeDtypeStruct((experts, 2 * ff, parts * LANES), jnp.float32),
            jax.ShapeDtypeStruct((8, length), jnp.float32),
        ]
        out_specs = [vmem_spec()] * 2
    return pl.pallas_call(
        functools.partial(expert_kernel, hops=hops, first=first, last=last, features=features),
        in_specs=in_specs,
        out_specs=out_specs,
        out_shape=out_shape,
        input_output_aliases=aliases,
        scratch_shapes=scratch,
        compiler_params=pltpu.CompilerParams(vmem_limit_bytes=36 * MIB),
        cost_estimate=pl.CostEstimate(
            flops=4 * experts * ff * parts * LANES * depth,
            bytes_accessed=4 * experts * ff * depth,
            transcendentals=0,
        ),
        name="expert_part",
    )(*operands)


def shards_by_heads(
    queries, keys, values, log_decay, state_in, norm_gain, routes, w_gate, w_up, n_seq, n_exp
):
    block, local_features = queries.shape
    features = n_exp * local_features
    length, chunk = n_seq * block, BLOCKS_A_PLANE * block
    parts = length // chunk
    experts = w_gate.shape[0]
    head_dim = state_in.shape[1]
    own = 3 * head_dim // 2
    rows = 3 * block + LOG_ROWS
    anywhere = pl.BlockSpec(memory_space=pl.ANY)

    def over_y(a):
        return lax.ppermute(a, "exp", [(e, e ^ 1) for e in range(n_exp)])

    def over_seq(a, hop):
        return lax.ppermute(a, "seq", [(s, s ^ hop) for s in range(n_seq)]) if hop else a

    def sibling(a):
        return over_seq(a, 1)

    def over_x(a):
        return over_seq(a, 2)

    def over_z(a, hop):
        return over_seq(a, 4 * hop)

    def together(*arrays):
        return lax.optimization_barrier(arrays)

    packed = pl.pallas_call(
        spread_kernel,
        in_specs=[vmem_spec()] * 5,
        out_specs=[vmem_spec()] * n_seq,
        out_shape=[jax.ShapeDtypeStruct((rows, 2 * head_dim), jnp.bfloat16)] * n_seq,
        compiler_params=pltpu.CompilerParams(vmem_limit_bytes=8 * MIB),
        name="spread",
    )(queries, keys, values, log_decay, routes.T)
    messages = [over_seq(a, hop) for hop, a in enumerate(packed)]
    x, final, named = pl.pallas_call(
        functools.partial(attend_kernel, block=block, chunk=chunk),
        in_specs=[vmem_spec()] * n_seq + [anywhere] * 2,
        out_specs=[vmem_spec()] * 3,
        out_shape=[
            jax.ShapeDtypeStruct((own + LOG_ROWS, length), jnp.bfloat16),
            jax.ShapeDtypeStruct((head_dim, 2 * head_dim), jnp.float32),
            jax.ShapeDtypeStruct((8, length), jnp.float32),
        ],
        scratch_shapes=[
            pltpu.VMEM((n_seq, rows, 2 * head_dim), jnp.bfloat16),
            pltpu.VMEM((3, head_dim, head_dim), jnp.float32),
            pltpu.VMEM((1, 2 * own), jnp.float32),
            pltpu.VMEM((head_dim, chunk), jnp.bfloat16),
            pltpu.SemaphoreType.DMA,
            pltpu.SemaphoreType.DMA,
            pltpu.VMEM((2, head_dim, head_dim), jnp.float32),
        ],
        compiler_params=pltpu.CompilerParams(vmem_limit_bytes=12 * MIB),
        name="attend",
    )(*messages, state_in, norm_gain.reshape(1, -1))
    select = pl.pallas_call(
        functools.partial(choose_kernel, experts=experts, block=block),
        in_specs=[vmem_spec()],
        out_specs=vmem_spec(),
        out_shape=jax.ShapeDtypeStruct((parts, chunk, experts * LANES), jnp.bfloat16),
        compiler_params=pltpu.CompilerParams(vmem_limit_bytes=8 * MIB),
        name="choose_rows",
    )(named)

    out_rows = head_dim // n_seq
    a, x0, y0, select, arrived = together(
        over_z(x, 1),
        over_x(x),
        over_y(x),
        select,
        lax.all_to_all(final.reshape(n_seq, out_rows, 2 * head_dim), "seq", 0, 0, tiled=True),
    )
    carry = None

    def call(hops, some, last=False):
        blocks = [one for block_of in some for one in (block_of, sibling(block_of))]
        return expert_part(hops, blocks, select, w_gate, w_up, carry, last, features)

    b, xa, ya, d0 = over_z(x, 2), over_x(a), over_y(a), over_y(x0)
    carry = call(((0, 0), (1, 0), (0, 1), (2, 0)), [x, x0, y0, a])
    b, xa, ya, d0, own, *carry = together(b, xa, ya, d0, x, *carry)
    c, xb, yb, da = over_z(own, 3), over_x(b), over_y(b), over_x(ya)
    carry = call(((3, 0), (2, 1), (1, 1), (4, 0)), [xa, ya, d0, b])
    c, xb, yb, da, *carry = together(c, xb, yb, da, *carry)
    xc, yc, db = over_x(c), over_y(c), over_x(yb)
    carry = call(((5, 0), (4, 1), (3, 1), (6, 0)), [xb, yb, da, c])
    dc = over_y(xc)
    carry = call(((7, 0), (6, 1), (5, 1)), [xc, yc, db])
    hidden = call(((7, 1),), [dc], True)
    state_out = pl.pallas_call(
        join_kernel,
        in_specs=[vmem_spec()],
        out_specs=vmem_spec(),
        out_shape=jax.ShapeDtypeStruct((state_in.shape[0], out_rows, head_dim), jnp.float32),
        compiler_params=pltpu.CompilerParams(vmem_limit_bytes=4 * MIB),
        name="join_state",
    )(arrived)
    return (hidden.swapaxes(1, 2), state_out)


def exchange_by_gathers(x, target, w_gate, w_up, n_seq, n_exp, group, planes, features):
    experts = w_gate.shape[0]
    width, length = x.shape[0] - LOG_ROWS, x.shape[1]
    every = lax.all_gather(x, ("seq", "exp")).reshape(planes, group, n_exp, -1, length)
    pieces = every[:, :, :, width : width + 3, :].astype(jnp.float32)
    token_scale = lax.rsqrt(jnp.sum(pieces, axis=(1, 2, 3)) / features + EPSILON)
    slots = group * CAP
    hit = target[:, :experts, None, :] == jnp.arange(slots)[None, None, :, None]

    def rows_of(pair):
        columns, chosen = pair
        columns = columns[:, :, :width, :].transpose(1, 0, 2, 3).reshape(features, length)
        return jnp.einsum("est,dt->esd", chosen.astype(jnp.bfloat16), columns)

    rows = lax.map(rows_of, (every, hit)).transpose(1, 0, 2, 3)
    rows = rows.reshape(experts, planes * slots, features)
    scale = jnp.sum(jnp.where(hit, token_scale[:, None, None, :], 0.0), axis=3)
    scale = scale.transpose(1, 0, 2).reshape(experts, 1, planes * slots)
    gate = jnp.einsum("efd,end->efn", w_gate, rows, preferred_element_type=jnp.float32) * scale
    up = jnp.einsum("efd,end->efn", w_up, rows, preferred_element_type=jnp.float32) * scale
    return (jax.nn.silu(gate) * up).astype(jnp.bfloat16)


def shards(queries, keys, values, log_decay, state_in, norm_gain, routes, w_gate, w_up, *, shape):
    n_seq, n_exp = shape["seq"], shape["exp"]
    if (n_seq, n_exp) == (16, 2) and 2 * state_in.shape[0] == 3 * n_seq:
        return shards_by_heads(
            queries,
            keys,
            values,
            log_decay,
            state_in,
            norm_gain,
            routes,
            w_gate,
            w_up,
            n_seq,
            n_exp,
        )
    block, features = queries.shape
    local_heads, head_dim = state_in.shape[0], state_in.shape[1]
    group = next(g for g in (4, 2, 1) if local_heads % g == 0 and n_seq % g == 0)
    planes = n_seq // group
    heads = local_heads // group
    length = group * block
    width = heads * head_dim
    def to_member(a, hop):
        if hop == 0:
            return a
        pairs = [(s, s // group * group + ((s % group) ^ hop)) for s in range(n_seq)]
        return lax.ppermute(a, "seq", pairs)

    def to_plane(a, shift):
        pairs = [((s), (s // group + shift) % planes * group + s % group) for s in range(n_seq)]
        return lax.ppermute(a, "seq", pairs)

    anywhere = pl.BlockSpec(memory_space=pl.ANY)
    *packed, own_state_in, own_gain = pl.pallas_call(
        functools.partial(pack_kernel, group=group),
        in_specs=[anywhere] * 5 + [vmem_spec()] * 2,
        out_specs=[vmem_spec()] * (2 * group + 2),
        out_shape=[jax.ShapeDtypeStruct((3 * block, width), jnp.bfloat16)] * group
        + [jax.ShapeDtypeStruct((8, block), jnp.float32)] * group
        + [
            jax.ShapeDtypeStruct((heads, head_dim, head_dim), jnp.float32),
            jax.ShapeDtypeStruct((1, width), jnp.float32),
        ],
        scratch_shapes=[pltpu.SemaphoreType.DMA((group + 1, 3))],
        compiler_params=pltpu.CompilerParams(vmem_limit_bytes=60 * MIB),
        name="pack",
    )(queries, keys, values, state_in, norm_gain.reshape(1, -1), log_decay, routes.T)
    messages = [to_member(packed[hop], hop) for hop in range(group)]
    logs = [to_member(packed[group + hop], hop) for hop in range(group)]

    whole = lambda *dims: pl.BlockSpec(dims, lambda i: (0,) * len(dims))
    query, inside, cumlog, own_state, message = pl.pallas_call(
        functools.partial(
            local_kernel, group=group, heads=heads, head_dim=head_dim, block=block
        ),
        grid=(1,),
        in_specs=[whole(3 * block, width)] * group + [whole(8, block)] * group,
        out_specs=[
            whole(length, width),
            whole(length, width),
            whole(length, 8),
            whole(heads, head_dim, head_dim),
            whole(heads, head_dim + LOG_ROWS, head_dim),
        ],
        out_shape=[
            jax.ShapeDtypeStruct((length, width), jnp.bfloat16),
            jax.ShapeDtypeStruct((length, width), jnp.float32),
            jax.ShapeDtypeStruct((length, 8), jnp.float32),
            jax.ShapeDtypeStruct((heads, head_dim, head_dim), jnp.float32),
            jax.ShapeDtypeStruct((heads, head_dim + LOG_ROWS, head_dim), jnp.bfloat16),
        ],
        scratch_shapes=[
            pltpu.VMEM((length, width), jnp.bfloat16),
            pltpu.VMEM((length, width), jnp.bfloat16),
            pltpu.VMEM((group, 8, block), jnp.float32),
        ],
        compiler_params=pltpu.CompilerParams(vmem_limit_bytes=16 * MIB),
        name="local_attention",
    )(*messages, *logs)
    arrived = [to_plane(message, shift) for shift in range(1, planes)]

    out_rows = head_dim // n_seq
    x, *pieces = pl.pallas_call(
        functools.partial(
            finish_kernel, planes=planes, group=group, heads=heads, head_dim=head_dim
        ),
        grid=(1,),
        in_specs=[whole(heads, head_dim + LOG_ROWS, head_dim)] * (planes - 1)
        + [
            whole(length, width),
            whole(length, width),
            whole(length, 8),
            whole(heads, head_dim, head_dim),
            whole(heads, head_dim, head_dim),
            whole(1, width),
        ],
        out_specs=[whole(width + LOG_ROWS, length)] + [whole(heads, out_rows, head_dim)] * group,
        out_shape=[jax.ShapeDtypeStruct((width + LOG_ROWS, length), jnp.bfloat16)]
        + [jax.ShapeDtypeStruct((heads, out_rows, head_dim), jnp.float32)] * group,
        scratch_shapes=[pltpu.VMEM((head_dim, head_dim), jnp.float32)],
        compiler_params=pltpu.CompilerParams(vmem_limit_bytes=20 * MIB),
        name="finish_attention",
    )(*arrived, query, inside, cumlog, own_state, own_state_in, own_gain)

    experts = w_gate.shape[0]
    target, select = pl.pallas_call(
        functools.partial(
            select_kernel, group=group, planes=planes, experts=experts, block=block, length=length
        ),
        grid=(1,),
        in_specs=[pl.BlockSpec((1, LOG_ROWS, head_dim), lambda i: (0, head_dim // LOG_ROWS, 0))] * planes,
        out_specs=[whole(planes, 8, length), whole(planes, length, experts * LANES)],
        out_shape=[
            jax.ShapeDtypeStruct((planes, 8, length), jnp.int32),
            jax.ShapeDtypeStruct((planes, length, experts * LANES), jnp.bfloat16),
        ],
        compiler_params=pltpu.CompilerParams(vmem_limit_bytes=12 * MIB),
        name="select_rows",
    )(message, *arrived)

    sizes = (n_seq, n_exp, group, planes, n_exp * features)
    hidden = exchange_by_gathers(x, target, w_gate, w_up, *sizes)

    pieces = [to_member(piece, hop) for hop, piece in enumerate(pieces)]
    state_out = pl.pallas_call(
        functools.partial(order_kernel, group=group, heads=heads),
        in_specs=[vmem_spec()] * group,
        out_specs=vmem_spec(),
        out_shape=jax.ShapeDtypeStruct((local_heads, out_rows, head_dim), jnp.float32),
        compiler_params=pltpu.CompilerParams(vmem_limit_bytes=4 * MIB),
        name="order_state",
    )(*pieces)
    return (hidden, state_out)


def solution(mesh):
    placed = (
        P("seq", "exp"),
        P("seq", "exp"),
        P("seq", "exp"),
        P("exp", "seq"),
        P("exp", None, None),
        P(),
        P("seq", None),
        P("exp", "seq", None),
        P("exp", "seq", None),
    )
    return jax.shard_map(
        functools.partial(shards, shape=dict(mesh.shape)),
        mesh=mesh,
        in_specs=placed,
        out_specs=(P("exp", "seq", None), P("exp", "seq", None)),
        check_vma=False,
    )
```
